128 devices in a mesh: grp: 4 (over z), rows: 32 (over y, x, core).
Axes of the slice: x: 4, y: 4, z: 4, core: 2. Of those that a mesh axis runs over, the one named last changes fastest.
Arguments:
- vectors: float32 [32768, 8192], P('rows', 'grp')
- column_a: float32 [32768, 384], P('rows'), as said below
- column_b: float32 [32768, 384], P('rows'), as said below
- pivot_a: int32 [384], replicated, may hold values from 0 to 32767, as said below
- pivot_b: int32 [384], replicated, may hold values from 0 to 32767, as said below
Outputs:
- new_a: float32 [32768, 384], P('rows', 'grp')
- new_b: float32 [32768, 384], P('rows', 'grp')
The draws below stay inside these ranges and needn't reach their ends.
Inputs may be any that keep to these rules, and one draw needn't show every extreme that they name: pivot_a and pivot_b together name 768 different pair rows, among them 0 and 32767. pivot_b names no row of pivot_a. `column_a`: residual_a[pivot_a] is positive definite. `column_b`: residual_b[pivot_b] is positive definite.
All inputs are finite; a program needn't handle non-finite values.
Results may differ from the reference program's by a relative error of at most 0.000058.
Values sent between devices are 32-bit elements; how exact they have to be, the bound alone decides.
No kernel may reach another device: no remote copies, remote signals or barrier semaphores. Data moves between devices by JAX's collectives and lax.ppermute only.
A program may use at most 128 MiB of HBM per device.

```python
import jax
import jax.numpy as jnp
from jax import lax

PANEL = 384
PAIRS = 32768
VECS = 8192


def shared_draw(key):
    middle = 1 + jax.random.permutation(jax.random.fold_in(key, 101), PAIRS - 2)[:2 * PANEL - 2]
    chosen = jnp.concatenate([jnp.array([0, PAIRS - 1], jnp.int32), middle.astype(jnp.int32)])
    order = jax.random.permutation(jax.random.fold_in(key, 102), 2 * PANEL)
    chosen = chosen[order]
    scale = 0.3 * VECS ** (-0.25)
    vectors = scale * jax.random.truncated_normal(jax.random.fold_in(key, 103), -6.0, 6.0, (PAIRS, VECS), jnp.float32)
    return (chosen[:PANEL], chosen[PANEL:], vectors)


def pivot_block_draw(key):
    spread = 4.8 / (PANEL - 1)
    offdiag = jax.random.uniform(jax.random.fold_in(key, 201), (PANEL, PANEL), jnp.float32, -spread, spread)
    diag = jax.random.uniform(jax.random.fold_in(key, 202), (PANEL,), jnp.float32, 6.0, 10.0)
    unit = jnp.eye(PANEL, dtype=jnp.float32)
    return offdiag * (1.0 - unit) + diag[None, :] * unit


def draw_vectors(key, part):
    first, second, vectors = shared_draw(key)
    return vectors


def draw_pivot_a(key, part):
    first, second, vectors = shared_draw(key)
    return first


def draw_pivot_b(key, part):
    first, second, vectors = shared_draw(key)
    return second


def draw_column_a(key, part):
    first, second, vectors = shared_draw(key)
    key = jax.random.fold_in(key, 11)
    base = 0.1 * jax.random.truncated_normal(jax.random.fold_in(key, 2), -6.0, 6.0, (PAIRS, PANEL), jnp.float32)
    coupling = 2.4 * PANEL ** (-0.5)
    linked = jax.random.uniform(jax.random.fold_in(key, 3), (PANEL, PANEL), jnp.float32, -coupling, coupling)
    base = base.at[second].set(linked)
    base = base.at[first].set(pivot_block_draw(jax.random.fold_in(key, 4)))
    return base + jnp.dot(vectors, vectors[first].T, precision=lax.Precision.HIGHEST, preferred_element_type=jnp.float32)


def draw_column_b(key, part):
    first, second, vectors = shared_draw(key)
    key = jax.random.fold_in(key, 12)
    base = 0.1 * jax.random.truncated_normal(jax.random.fold_in(key, 2), -6.0, 6.0, (PAIRS, PANEL), jnp.float32)
    base = base.at[second].set(pivot_block_draw(jax.random.fold_in(key, 4)))
    return base + jnp.dot(vectors, vectors[second].T, precision=lax.Precision.HIGHEST, preferred_element_type=jnp.float32)


def setup_inputs(seed: int = 0) -> dict:
    streams_of = jax.random.split(jax.random.key(seed), 6)
    return {
        "vectors": draw_vectors(jax.random.fold_in(streams_of[5], 71), 0),
        "column_a": draw_column_a(jax.random.fold_in(streams_of[5], 71), 0),
        "column_b": draw_column_b(jax.random.fold_in(streams_of[5], 71), 0),
        "pivot_a": draw_pivot_a(jax.random.fold_in(streams_of[5], 71), 0),
        "pivot_b": draw_pivot_b(jax.random.fold_in(streams_of[5], 71), 0),
    }


def exact_dot(left, right):
    return jnp.dot(left.astype(jnp.float32), right.astype(jnp.float32), precision=lax.Precision.HIGHEST, preferred_element_type=jnp.float32)

def panel_factor(residual, pivots):
    pivot_block = residual[pivots]
    factor_low = jnp.linalg.cholesky(pivot_block)
    return jax.scipy.linalg.solve_triangular(factor_low, residual.T, lower=True).T

def reference(vectors, column_a, column_b, pivot_a, pivot_b):
    residual_a = column_a - exact_dot(vectors, vectors[pivot_a].T)
    new_a = panel_factor(residual_a, pivot_a)
    residual_b = column_b - exact_dot(vectors, vectors[pivot_b].T) - exact_dot(new_a, new_a[pivot_b].T)
    new_b = panel_factor(residual_b, pivot_b)
    return (new_a, new_b)
```

```python
import functools

import jax
import jax.numpy as jnp
from jax import lax
from jax.experimental import pallas as pl
from jax.experimental.pallas import tpu as pltpu
from jax.sharding import PartitionSpec as P

HIGHEST = lax.Precision.HIGHEST
CAP = 32
COMES_FROM = (0, 1, 3, 2)
VMEM = pltpu.VMEM
LIMIT = 50 * 1024 * 1024


def vmem():
    return pl.BlockSpec(memory_space=VMEM)


def smem():
    return pl.BlockSpec(memory_space=pltpu.SMEM)


def params():
    return pltpu.CompilerParams(vmem_limit_bytes=LIMIT)


def cost(flops, byte_count):
    return pl.CostEstimate(flops=flops, bytes_accessed=byte_count, transcendentals=0)


def nt(left, right, precision=HIGHEST):
    return lax.dot_general(
        left, right, (((1,), (1,)), ((), ())), precision=precision, preferred_element_type=jnp.float32
    )


def nn(left, right):
    return lax.dot_general(
        left, right, (((1,), (0,)), ((), ())), precision=HIGHEST, preferred_element_type=jnp.float32
    )


def tn(left, right):
    return lax.dot_general(
        left, right, (((0,), (0,)), ((), ())), precision=HIGHEST, preferred_element_type=jnp.float32
    )


def pick_kernel(rows_ref, v_ref, ca_ref, cb_ref, out_ref, vbuf, abuf, bbuf, sems):
    count = vbuf.shape[0]

    @pl.loop(0, count)
    def _(slot):
        row = rows_ref[slot]
        pltpu.make_async_copy(v_ref.at[pl.ds(row, 1)], vbuf.at[pl.ds(slot, 1)], sems.at[0]).start()
        pltpu.make_async_copy(ca_ref.at[pl.ds(row, 1)], abuf.at[pl.ds(slot, 1)], sems.at[1]).start()
        pltpu.make_async_copy(cb_ref.at[pl.ds(row, 1)], bbuf.at[pl.ds(slot, 1)], sems.at[2]).start()

    pltpu.make_async_copy(vbuf, vbuf, sems.at[0]).wait()
    pltpu.make_async_copy(abuf, abuf, sems.at[1]).wait()
    pltpu.make_async_copy(bbuf, bbuf, sems.at[2]).wait()
    half = CAP // 2
    gap = jnp.zeros((half, 16), jnp.float32)
    for q in range(2):
        for c in range(16):
            out_ref[2 * c + q, 0:CAP, :] = vbuf[q * CAP : (q + 1) * CAP, 128 * c : 128 * c + 128]
            source = abuf if c < 8 else bbuf
            start = 48 * (c % 8)
            low = source[q * CAP : q * CAP + half, start : start + 48]
            high = source[q * CAP + half : (q + 1) * CAP, start : start + 48]
            out_ref[2 * c + q, CAP : CAP + half, :] = jnp.concatenate([low, gap, high, gap], axis=1)


def pick(rows, vectors, column_a, column_b):
    width = vectors.shape[1]
    anywhere = pl.BlockSpec(memory_space=pl.ANY)
    return pl.pallas_call(
        pick_kernel,
        out_shape=jax.ShapeDtypeStruct((32, CAP + CAP // 2, 128), jnp.float32),
        in_specs=[smem(), anywhere, anywhere, anywhere],
        out_specs=vmem(),
        scratch_shapes=[
            VMEM((2 * CAP, width), jnp.float32),
            VMEM((2 * CAP, 384), jnp.float32),
            VMEM((2 * CAP, 384), jnp.float32),
            pltpu.SemaphoreType.DMA((3,)),
        ],
        compiler_params=params(),
        name="pick_rows",
    )(rows, vectors, column_a, column_b)


def place_kernel(pos_ref, flag_ref, got_ref, x_ref, colt_ref, cbuf):
    @pl.loop(0, 384, unroll=8)
    def _(i):
        owner, slot = pos_ref[0, i], pos_ref[1, i]
        x_ref[pl.ds(i, 1), :] = got_ref[owner, pl.ds(slot, 1), :]
        cbuf[pl.ds(i, 1), :] = got_ref[owner, pl.ds(CAP + lax.rem(slot, CAP // 2), 1), :]

    packed = cbuf[...]
    chosen = jnp.where(flag_ref[...] > 0, packed[:, 64:112], packed[:, 0:48])
    colt_ref[...] = chosen.T


def place(pos, high, got):
    return pl.pallas_call(
        place_kernel,
        out_shape=(
            jax.ShapeDtypeStruct((384, 128), jnp.float32),
            jax.ShapeDtypeStruct((48, 384), jnp.float32),
        ),
        in_specs=[smem(), vmem(), vmem()],
        out_specs=(vmem(), vmem()),
        scratch_shapes=[VMEM((384, 128), jnp.float32)],
        compiler_params=params(),
        name="place_rows",
    )(pos, high, got)


def turned(axis, step):
    def to(index):
        y, x, core = index // 8, (index // 2) % 4, index % 2
        along_x = axis == "x" if core == 0 else axis == "y"
        if along_x:
            x = (x + step) % 4
        else:
            y = (y + step) % 4
        return (y * 4 + x) * 2 + core

    return [(index, to(index)) for index in range(32)]


def other_core(array):
    return lax.ppermute(array, "rows", [(index, index ^ 1) for index in range(32)])


def plane_gather(block):
    near = [block] + [lax.ppermute(block, "rows", turned("x", step)) for step in COMES_FROM[1:]]
    line = jnp.stack(near)
    lines = [line] + [lax.ppermute(line, "rows", turned("y", step)) for step in COMES_FROM[1:]]
    return lines + [other_core(line) for line in lines]


def spots(place_ref):
    y, x, core = place_ref[0], place_ref[1], place_ref[2]
    found = []
    for array in range(8):
        q = core if array < 4 else 1 - core
        outer = COMES_FROM[array % 4]
        for piece in range(4):
            inner = COMES_FROM[piece]
            dx = jnp.where(q == 0, inner, outer)
            dy = jnp.where(q == 0, outer, inner)
            chip = lax.rem(y + 4 - dy, 4) * 4 + lax.rem(x + 4 - dx, 4)
            found.append((array, piece, chip, q))
    return found


def order_kernel(place_ref, *refs):
    arrays, colt_ref, high_ref, low_ref, tile_ref, whole = refs[:8], refs[8], refs[9], refs[10], refs[11], refs[12]
    for array, piece, chip, q in spots(place_ref):
        lanes = pl.ds(pl.multiple_of(chip * 128, 128), 128)
        for panel in range(2):
            rows = pl.ds(pl.multiple_of(384 * panel + 192 * q, 64), 192)
            block = arrays[array][piece, 192 * panel : 192 * panel + 192, :]
            whole[rows, lanes] = block
            high = block.astype(jnp.bfloat16)
            high_ref[rows, lanes] = high
            low_ref[rows, lanes] = (block - high.astype(jnp.float32)).astype(jnp.bfloat16)
    core = place_ref[2]
    mine = whole[pl.ds(pl.multiple_of((place_ref[0] * 4 + place_ref[1]) * 48, 16), 48), :]
    for panel in range(2):
        rows = pl.ds(pl.multiple_of(384 * panel + 192 * core, 64), 192)
        span = slice(192 * panel, 192 * panel + 192)
        tile_ref[:, span] = 0.25 * colt_ref[:, span] - nt(mine, whole[rows, :])


def order(where, lines, colt):
    return pl.pallas_call(
        order_kernel,
        out_shape=(
            jax.ShapeDtypeStruct((768, 2048), jnp.bfloat16),
            jax.ShapeDtypeStruct((768, 2048), jnp.bfloat16),
            jax.ShapeDtypeStruct((48, 384), jnp.float32),
        ),
        in_specs=[smem()] + [vmem()] * 9,
        out_specs=(vmem(), vmem(), vmem()),
        scratch_shapes=[VMEM((768, 2048), jnp.float32)],
        compiler_params=params(),
        cost_estimate=cost(2 * 48 * 384 * 2048 * 6, 12 * 768 * 2048),
        name="order_rows",
    )(where, *lines, colt)


def product_kernel(chunk_ref, v_ref, ca_ref, cb_ref, high_ref, low_ref, out_ref, vhigh, vlow):
    step = pl.program_id(0)

    @pl.when(step == 0)
    def _():
        value = v_ref[...]
        high = value.astype(jnp.bfloat16)
        vhigh[...] = high
        vlow[...] = (value - high.astype(jnp.float32)).astype(jnp.bfloat16)

    total = nt(vhigh[...], high_ref[...], None)
    total += nt(vhigh[...], low_ref[...], None)
    total += nt(vlow[...], high_ref[...], None)
    column = jnp.where(step == 0, ca_ref[...], cb_ref[...])
    out_ref[...] = 0.25 * column - total


def product(chunk, vectors, column_a, column_b, high, low):
    size = vectors.shape[0] // 4
    width = vectors.shape[1]
    return pl.pallas_call(
        product_kernel,
        out_shape=jax.ShapeDtypeStruct((size, 768), jnp.float32),
        grid_spec=pltpu.PrefetchScalarGridSpec(
            num_scalar_prefetch=1,
            grid=(2,),
            in_specs=[
                pl.BlockSpec((size, width), lambda n, chunk: (chunk[0], 0)),
                pl.BlockSpec((size, 384), lambda n, chunk: (chunk[0], 0)),
                pl.BlockSpec((size, 384), lambda n, chunk: (chunk[0], 0)),
                pl.BlockSpec((384, width), lambda n, chunk: (n, 0)),
                pl.BlockSpec((384, width), lambda n, chunk: (n, 0)),
            ],
            out_specs=pl.BlockSpec((size, 384), lambda n, chunk: (0, n)),
            scratch_shapes=[VMEM((size, width), jnp.bfloat16), VMEM((size, width), jnp.bfloat16)],
        ),
        compiler_params=params(),
        cost_estimate=cost(2 * 3 * size * width * 768, 4 * size * width + 4 * 768 * width),
        name="product_rows",
    )(chunk, vectors, column_a, column_b, high, low)


def spread(row, index):
    return jnp.broadcast_to(row[index : index + 1, :], (8, 128))


def invert_factor(a):
    row_of = lax.broadcasted_iota(jnp.int32, (8, 128), 0)
    lane_of = lax.broadcasted_iota(jnp.int32, (8, 128), 1)
    e = [jnp.where(lane_of == row_of + 8 * j, 1.0, 0.0) for j in range(16)]
    done = []
    for j in range(16):
        rest = range(j, 16)
        cols = {
            (s, i): jnp.broadcast_to(a[s][:, 8 * j + i : 8 * j + i + 1], (8, 128)) for s in rest for i in range(8)
        }
        diagonal = jnp.ones((8, 128), jnp.float32)
        for i in range(8):
            pivot = spread(cols[(j, i)], i)
            diagonal = jnp.where(row_of == i, pivot, diagonal)
            inverse = 1.0 / pivot
            factor = {s: cols[(s, i)] * inverse for s in rest}
            factor[j] = jnp.where(row_of > i, factor[j], 0.0)
            for later in range(i + 1, 8):
                head = spread(cols[(j, later)], i)
                for s in rest:
                    cols[(s, later)] = cols[(s, later)] - factor[s] * head
            head_a, head_e = spread(a[j], i), spread(e[j], i)
            for s in rest:
                a[s] = a[s] - factor[s] * head_a
                e[s] = e[s] - factor[s] * head_e
        done.append(e[j] * lax.rsqrt(diagonal))
    return done


def panel_inverse(s, w):
    w[...] = jnp.zeros_like(w)
    for b in range(3):
        here = slice(128 * b, 128 * b + 128)
        strips = invert_factor([s[128 * b + 8 * j : 128 * b + 8 * j + 8, here] for j in range(16)])
        for j in range(16):
            w[128 * b + 8 * j : 128 * b + 8 * j + 8, here] = strips[j]
        inverse = w[here, here]
        if b:
            w[here, : 128 * b] = nn(inverse, w[here, : 128 * b])
        if b < 2:
            below = slice(128 * b + 128, 384)
            left = nt(s[below, here], inverse)
            s[below, below] = s[below, below] - nt(left, left)
            w[below, : 128 * b + 128] = w[below, : 128 * b + 128] - nn(left, w[here, : 128 * b + 128])


def factor_kernel(place_ref, *refs):
    arrays, wa, wb, nba, st, s = refs[:8], refs[8], refs[9], refs[10], refs[11], refs[12]
    for array, piece, chip, q in spots(place_ref):
        st[q, pl.ds(pl.multiple_of(chip * 48, 16), 48), :] = arrays[array][piece]

    def block(first_row, first_lane):
        rows, lanes = slice(first_row, first_row + 384), slice(first_lane, first_lane + 192)
        return jnp.concatenate([st[0, rows, lanes], st[1, rows, lanes]], axis=1)

    aa = block(0, 0)
    s[...] = 0.5 * (aa + aa.T)
    panel_inverse(s, wa)
    nba[...] = nn(wa[...], block(0, 192))
    bb = block(384, 192)
    s[...] = 0.5 * (bb + bb.T) - tn(nba[...], nba[...])
    panel_inverse(s, wb)


def factors(where, lines):
    square = jax.ShapeDtypeStruct((384, 384), jnp.float32)
    return pl.pallas_call(
        factor_kernel,
        out_shape=(square, square, square),
        in_specs=[smem()] + [vmem()] * 8,
        out_specs=(vmem(), vmem(), vmem()),
        scratch_shapes=[VMEM((2, 768, 384), jnp.float32), VMEM((384, 384), jnp.float32)],
        compiler_params=params(),
        cost_estimate=cost(2 * 10 * 768 * 768 * 768, 20 * 384 * 384),
        name="pivot_factors",
    )(where, *lines)


def finish_kernel(place_ref, r0, r1, r2, r3, wa_ref, wb_ref, nba_ref, p0, p1, p2, p3, wide_a, wide_b):
    total = (r0[...] + r1[...]) + (r2[...] + r3[...])
    left, right = total[:, :384], total[:, 384:]
    new_a = nt(left, wa_ref[...])
    right = right - nn(new_a, nba_ref[...])
    wide_a[...] = left
    wide_b[...] = right
    for hop, out in zip(COMES_FROM, (p0, p1, p2, p3)):
        rows = pl.ds(pl.multiple_of(lax.rem(place_ref[3] + hop, 4) * 96, 32), 96)
        out[0] = nt(wide_a[...], wa_ref[rows, :])
        out[1] = nt(wide_b[...], wb_ref[rows, :])


def finish(where, parts, wa, wb, nba):
    size = parts[0].shape[0]
    piece = jax.ShapeDtypeStruct((2, size, 96), jnp.float32)
    return pl.pallas_call(
        finish_kernel,
        out_shape=(piece,) * 4,
        in_specs=[smem()] + [vmem()] * 7,
        out_specs=(vmem(),) * 4,
        scratch_shapes=[VMEM((size, 384), jnp.float32), VMEM((size, 384), jnp.float32)],
        compiler_params=params(),
        cost_estimate=cost(2 * 6 * size * 384 * 384 * 4, 4 * size * 768 * 6),
        name="new_vectors",
    )(where, *parts, wa, wb, nba)


def join_kernel(place_ref, p0, p1, p2, p3, a_ref, b_ref):
    size = p0.shape[1]
    for hop, piece in zip(COMES_FROM, (p0, p1, p2, p3)):
        rows = pl.ds(pl.multiple_of(lax.rem(place_ref[3] + 4 - hop, 4) * size, size), size)
        a_ref[rows, :] = piece[0]
        b_ref[rows, :] = piece[1]


def join(where, pieces):
    size = pieces[0].shape[1]
    out = jax.ShapeDtypeStruct((4 * size, 96), jnp.float32)
    return pl.pallas_call(
        join_kernel,
        out_shape=(out, out),
        in_specs=[smem()] + [vmem()] * 4,
        out_specs=(vmem(), vmem()),
        compiler_params=params(),
        name="join_vectors",
    )(where, *pieces)


def to_group(array, hop):
    return lax.ppermute(array, "grp", [(g, (g + hop) % 4) for g in range(4)])


def body(vectors, column_a, column_b, pivot_a, pivot_b):
    rows_here = vectors.shape[0]
    place_here = lax.axis_index("rows")
    group = lax.axis_index("grp")
    core = place_here % 2
    where = jnp.stack([place_here // 8, (place_here // 2) % 4, core, group]).astype(jnp.int32)

    halves = jnp.concatenate([pivot_a.reshape(2, 192), pivot_b.reshape(2, 192)], axis=1)
    owner, local = halves // rows_here, halves % rows_here
    index = lax.iota(jnp.int32, 384)
    same = (owner[:, :, None] == owner[:, None, :]) & (index[None, :, None] > index[None, None, :])
    rank = jnp.sum(same.astype(jnp.int32), axis=2)
    rounds = jnp.max(rank) // CAP + 1
    owner_q = lax.dynamic_index_in_dim(owner, core, 0, False)
    rank_q = lax.dynamic_index_in_dim(rank, core, 0, False)

    def one_round(turn):
        slots = turn * CAP + lax.iota(jnp.int32, CAP)
        hit = (owner == place_here)[:, None, :] & (rank[:, None, :] == slots[None, :, None])
        rows = jnp.sum(jnp.where(hit, local[:, None, :], 0), axis=2).reshape(2 * CAP)
        sent = pick(rows, vectors, column_a, column_b)
        got = lax.all_to_all(sent, "rows", 0, 0)
        slot_q = jnp.clip(rank_q - turn * CAP, 0, CAP - 1)
        high = (slot_q >= CAP // 2).astype(jnp.int32)[:, None]
        return place(jnp.stack([owner_q, slot_q]), high, got)

    def more(state):
        turn, block, colt = state
        new_block, new_colt = one_round(turn)
        now = rank_q // CAP == turn
        return turn + 1, jnp.where(now[:, None], new_block, block), jnp.where(now[None, :], new_colt, colt)

    block, colt = one_round(0)
    _, block, colt = lax.while_loop(lambda state: state[0] < rounds, more, (jnp.int32(1), block, colt))

    high, low, tile = order(where, plane_gather(block), colt)
    parts = {}
    sums = [tile] + [to_group(tile, hop) for hop in COMES_FROM[1:]]
    tile = (sums[0] + sums[1]) + (sums[2] + sums[3])
    tiles = plane_gather(tile)
    for hop in COMES_FROM:
        chunk = ((group + hop) % 4).astype(jnp.int32)[None]
        parts[hop] = product(chunk, vectors, column_a, column_b, high, low)
    total = [parts[0]] + [to_group(parts[hop], hop) for hop in COMES_FROM[1:]]
    wa, wb, nba = factors(where, tiles)
    pieces = finish(where, total, wa, wb, nba)
    pieces = [pieces[0]] + [to_group(piece, hop) for hop, piece in zip(COMES_FROM[1:], pieces[1:])]
    return join(where, pieces)


def solution(mesh):
    in_specs = (P("rows", "grp"), P("rows", None), P("rows", None), P(), P())
    out_specs = (P("rows", "grp"), P("rows", "grp"))
    return jax.shard_map(body, mesh=mesh, in_specs=in_specs, out_specs=out_specs, check_vma=False)
```

```python
import functools

import jax
import jax.numpy as jnp
from jax import lax
from jax.experimental import pallas as pl
from jax.experimental.pallas import tpu as pltpu
from jax.sharding import PartitionSpec as P

HIGHEST = lax.Precision.HIGHEST
CAP = 48
COMES_FROM = (0, 1, 3, 2)
VMEM = pltpu.VMEM
LIMIT = 50 * 1024 * 1024


def vmem():
    return pl.BlockSpec(memory_space=VMEM)


def smem():
    return pl.BlockSpec(memory_space=pltpu.SMEM)


def params():
    return pltpu.CompilerParams(vmem_limit_bytes=LIMIT)


def cost(flops, byte_count):
    return pl.CostEstimate(flops=flops, bytes_accessed=byte_count, transcendentals=0)


def nt(left, right, precision=HIGHEST):
    return lax.dot_general(
        left, right, (((1,), (1,)), ((), ())), precision=precision, preferred_element_type=jnp.float32
    )


def nn(left, right):
    return lax.dot_general(
        left, right, (((1,), (0,)), ((), ())), precision=HIGHEST, preferred_element_type=jnp.float32
    )


def tn(left, right):
    return lax.dot_general(
        left, right, (((0,), (0,)), ((), ())), precision=HIGHEST, preferred_element_type=jnp.float32
    )


def pick_kernel(rows_ref, v_ref, ca_ref, cb_ref, out_ref, vbuf, abuf, bbuf, sems):
    count = vbuf.shape[0]

    @pl.loop(0, count)
    def _(slot):
        row = rows_ref[slot]
        pltpu.make_async_copy(v_ref.at[pl.ds(row, 1)], vbuf.at[pl.ds(slot, 1)], sems.at[0]).start()
        pltpu.make_async_copy(ca_ref.at[pl.ds(row, 1)], abuf.at[pl.ds(slot, 1)], sems.at[1]).start()
        pltpu.make_async_copy(cb_ref.at[pl.ds(row, 1)], bbuf.at[pl.ds(slot, 1)], sems.at[2]).start()

    pltpu.make_async_copy(vbuf, vbuf, sems.at[0]).wait()
    pltpu.make_async_copy(abuf, abuf, sems.at[1]).wait()
    pltpu.make_async_copy(bbuf, bbuf, sems.at[2]).wait()
    gap = jnp.zeros((CAP, 40), jnp.float32)
    for c in range(16):
        for q, column in enumerate((abuf, bbuf)):
            start = 128 * c + 64 * q
            out_ref[2 * c + q] = jnp.concatenate(
                [vbuf[:, start : start + 64], column[:, 24 * c : 24 * c + 24], gap], axis=1
            )


def pick(rows, vectors, column_a, column_b):
    width = vectors.shape[1]
    anywhere = pl.BlockSpec(memory_space=pl.ANY)
    return pl.pallas_call(
        pick_kernel,
        out_shape=jax.ShapeDtypeStruct((32, CAP, 128), jnp.float32),
        in_specs=[smem(), anywhere, anywhere, anywhere],
        out_specs=vmem(),
        scratch_shapes=[
            VMEM((CAP, width), jnp.float32),
            VMEM((CAP, 384), jnp.float32),
            VMEM((CAP, 384), jnp.float32),
            pltpu.SemaphoreType.DMA((3,)),
        ],
        compiler_params=params(),
        name="pick_rows",
    )(rows, vectors, column_a, column_b)


def place_kernel(pos_ref, got_ref, x_ref, colt_ref, buf):
    @pl.loop(0, 768, unroll=8)
    def _(i):
        buf[pl.ds(i, 1), :] = got_ref[pos_ref[0, i], pl.ds(pos_ref[1, i], 1), :]

    x_ref[...] = jnp.concatenate([buf[:384, :64], buf[384:, :64]], axis=1)
    colt_ref[...] = buf[:, 64:88].T


def place(pos, got):
    return pl.pallas_call(
        place_kernel,
        out_shape=(
            jax.ShapeDtypeStruct((384, 128), jnp.float32),
            jax.ShapeDtypeStruct((24, 768), jnp.float32),
        ),
        in_specs=[smem(), vmem()],
        out_specs=(vmem(), vmem()),
        scratch_shapes=[VMEM((768, 128), jnp.float32)],
        compiler_params=params(),
        name="place_rows",
    )(pos, got)


def turned(axis, step):
    def to(index):
        y, x, core = index // 8, (index // 2) % 4, index % 2
        along_x = axis == "x" if core == 0 else axis == "y"
        if along_x:
            x = (x + step) % 4
        else:
            y = (y + step) % 4
        return (y * 4 + x) * 2 + core

    return [(index, to(index)) for index in range(32)]


def paired(axis, bit):
    def to(index):
        y, x, core = index // 8, (index // 2) % 4, index % 2
        along_x = axis == "x" if core == 0 else axis == "y"
        return ((y * 4 + (x ^ bit)) if along_x else ((y ^ bit) * 4 + x)) * 2 + core

    return [(index, to(index)) for index in range(32)]


def other_core(array):
    return lax.ppermute(array, "rows", [(index, index ^ 1) for index in range(32)])


def first_ring(block):
    return jnp.stack([block] + [lax.ppermute(block, "rows", turned("x", step)) for step in COMES_FROM[1:]])


def second_ring(line):
    return [line] + [lax.ppermute(line, "rows", turned("y", step)) for step in COMES_FROM[1:]]


def flipped(value, bit):
    low = value + (bit % 2) * (1 - 2 * lax.rem(value, 2))
    return lax.rem(low + 2 * (bit // 2), 4)


def spot_flipped(place_ref, outer, inner):
    y, x, core = place_ref[0], place_ref[1], place_ref[2]
    at_x = jnp.where(core == 0, flipped(x, inner), lax.rem(x + 4 - outer, 4))
    at_y = jnp.where(core == 0, lax.rem(y + 4 - outer, 4), flipped(y, inner))
    return at_y * 4 + at_x


def spot(place_ref, outer, inner):
    y, x, core = place_ref[0], place_ref[1], place_ref[2]
    dx = jnp.where(core == 0, inner, outer)
    dy = jnp.where(core == 0, outer, inner)
    return lax.rem(y + 4 - dy, 4) * 4 + lax.rem(x + 4 - dx, 4)


def share_kernel(place_ref, line_ref, colt_ref, o0, o1, far, first, second):
    for piece in range(4):
        value = line_ref[piece]
        first[:, 64 * piece : 64 * piece + 64] = value[:, :64]
        second[:, 64 * piece : 64 * piece + 64] = value[:, 64:]
    rows_a, rows_b = [], []
    y, x, core = place_ref[0], place_ref[1], place_ref[2]
    for bit in range(4):
        chip = jnp.where(core == 0, flipped(y, bit) * 4 + x, y * 4 + flipped(x, bit))
        rows = pl.ds(pl.multiple_of(chip * 24, 8), 24)
        rows_a.append(first[rows, :])
        rows_b.append(second[rows, :])
    rows_a, rows_b = jnp.concatenate(rows_a, axis=0), jnp.concatenate(rows_b, axis=0)
    aa, ab, bb = nt(rows_a, first[...]), nt(rows_a, second[...]), nt(rows_b, second[...])
    for number, out in enumerate((o0, o1, far.at[0], far.at[1])):
        some = slice(24 * number, 24 * number + 24)
        out[:, :384] = -aa[some]
        out[:, 384:768] = -ab[some]
        out[:, 768:] = -bb[some]

    @pl.when(core == 0)
    def _():
        o0[:, :768] += 0.25 * colt_ref[...]

    @pl.when(core == 1)
    def _():
        o0[:, 768:] += 0.25 * colt_ref[:, 384:]


def share(where, line, colt):
    return pl.pallas_call(
        share_kernel,
        out_shape=(
            jax.ShapeDtypeStruct((24, 1152), jnp.float32),
            jax.ShapeDtypeStruct((24, 1152), jnp.float32),
            jax.ShapeDtypeStruct((2, 24, 1152), jnp.float32),
        ),
        in_specs=[smem(), vmem(), vmem()],
        out_specs=(vmem(),) * 3,
        scratch_shapes=[VMEM((384, 256), jnp.float32), VMEM((384, 256), jnp.float32)],
        compiler_params=params(),
        cost_estimate=cost(2 * 96 * 1152 * 256 * 24, 4 * 384 * 512),
        name="pivot_share",
    )(where, line, colt)


def split(value):
    high = value.astype(jnp.bfloat16)
    return high, (value - high.astype(jnp.float32)).astype(jnp.bfloat16)


def order_rows(place_ref, own, sibling, high_ref, low_ref):
    for outer in range(4):
        for inner in range(4):
            lanes = pl.ds(pl.multiple_of(spot(place_ref, COMES_FROM[outer], COMES_FROM[inner]) * 128, 128), 128)
            mine, theirs = own[outer][inner], sibling[inner][outer]
            low_core = jnp.where(place_ref[2] == 0, mine, theirs)
            high_core = jnp.where(place_ref[2] == 0, theirs, mine)
            for panel in range(2):
                half = slice(64 * panel, 64 * panel + 64)
                tile = jnp.concatenate([low_core[:, half], high_core[:, half]], axis=1)
                rows = slice(384 * panel, 384 * panel + 384)
                high_ref[rows, lanes], low_ref[rows, lanes] = split(tile)


def split_kernel(v_ref, high_ref, low_ref):
    high_ref[...], low_ref[...] = split(v_ref[...])


def split_rows(vectors):
    rows, width = vectors.shape
    block = pl.BlockSpec((rows // 8, width), lambda n: (n, 0))
    half = jax.ShapeDtypeStruct((rows, width), jnp.bfloat16)
    return pl.pallas_call(
        split_kernel,
        out_shape=(half, half),
        grid=(8,),
        in_specs=[block],
        out_specs=(block, block),
        compiler_params=params(),
        cost_estimate=cost(4 * rows * width, 8 * rows * width),
        name="split_vectors",
    )(vectors)


def product_kernel(place_ref, vhigh, vlow, ca_ref, cb_ref, *refs):
    own, sibling, outs, high_ref, low_ref = refs[:4], refs[4:8], refs[8:12], refs[12], refs[13]
    step = pl.program_id(0)

    @pl.when(step == 0)
    def _():
        order_rows(place_ref, own, sibling, high_ref, low_ref)

    total = nt(vhigh[...], high_ref[...], None)
    total += nt(vhigh[...], low_ref[...], None)
    total += nt(vlow[...], high_ref[...], None)
    for number, out in enumerate(outs):

        @pl.when(step == number)
        def _():
            out[:, :384] = 0.25 * ca_ref[...] - total[:, :384]
            out[:, 384:] = 0.25 * cb_ref[...] - total[:, 384:]


def product(where, vhigh, vlow, column_a, column_b, lines):
    rows, width = vhigh.shape
    size = rows // 4

    def chunk(n, place):
        hop = jnp.where(n < 2, n, 5 - n)
        return lax.rem(place[3] + hop, 4), 0

    whole = pl.BlockSpec(lines[0].shape, lambda n, place: (0, 0, 0))
    return pl.pallas_call(
        product_kernel,
        out_shape=(jax.ShapeDtypeStruct((size, 768), jnp.float32),) * 4,
        grid_spec=pltpu.PrefetchScalarGridSpec(
            num_scalar_prefetch=1,
            grid=(4,),
            in_specs=[
                pl.BlockSpec((size, width), chunk),
                pl.BlockSpec((size, width), chunk),
                pl.BlockSpec((size, 384), chunk),
                pl.BlockSpec((size, 384), chunk),
            ]
            + [whole] * 8,
            out_specs=(pl.BlockSpec((size, 768), lambda n, place: (0, 0)),) * 4,
            scratch_shapes=[VMEM((768, width), jnp.bfloat16), VMEM((768, width), jnp.bfloat16)],
        ),
        compiler_params=params(),
        cost_estimate=cost(2 * 3 * rows * width * 768, 4 * rows * width + 4 * 768 * width),
        name="product_rows",
    )(where, vhigh, vlow, column_a, column_b, *lines)


def spread(row, index):
    return jnp.broadcast_to(row[index : index + 1, :], (8, 128))


def invert_factor(a):
    row_of = lax.broadcasted_iota(jnp.int32, (8, 128), 0)
    lane_of = lax.broadcasted_iota(jnp.int32, (8, 128), 1)
    e = [jnp.where(lane_of == row_of + 8 * j, 1.0, 0.0) for j in range(16)]
    done = []
    for j in range(16):
        rest = range(j, 16)
        cols = {
            (s, i): jnp.broadcast_to(a[s][:, 8 * j + i : 8 * j + i + 1], (8, 128)) for s in rest for i in range(8)
        }
        diagonal = jnp.ones((8, 128), jnp.float32)
        for i in range(8):
            pivot = spread(cols[(j, i)], i)
            diagonal = jnp.where(row_of == i, pivot, diagonal)
            inverse = 1.0 / pivot
            factor = {s: cols[(s, i)] * inverse for s in rest}
            factor[j] = jnp.where(row_of > i, factor[j], 0.0)
            for later in range(i + 1, 8):
                head = spread(cols[(j, later)], i)
                for s in rest:
                    cols[(s, later)] = cols[(s, later)] - factor[s] * head
            head_a, head_e = spread(a[j], i), spread(e[j], i)
            for s in rest:
                a[s] = a[s] - factor[s] * head_a
                e[s] = e[s] - factor[s] * head_e
        done.append(e[j] * lax.rsqrt(diagonal))
    return done


def panel_inverse(s, w):
    w[...] = jnp.zeros_like(w)
    for b in range(3):
        here = slice(128 * b, 128 * b + 128)
        strips = invert_factor([s[128 * b + 8 * j : 128 * b + 8 * j + 8, here] for j in range(16)])
        for j in range(16):
            w[128 * b + 8 * j : 128 * b + 8 * j + 8, here] = strips[j]
        inverse = w[here, here]
        if b:
            w[here, : 128 * b] = nn(inverse, w[here, : 128 * b])
        if b < 2:
            below = slice(128 * b + 128, 384)
            left = nt(s[below, here], inverse)
            s[below, below] = s[below, below] - nt(left, left)
            w[below, : 128 * b + 128] = w[below, : 128 * b + 128] - nn(left, w[here, : 128 * b + 128])


def sort_tiles(place_ref, lines, st, lanes):
    for outer in range(4):
        for inner in range(4):
            chip = spot_flipped(place_ref, COMES_FROM[outer], inner)
            st[pl.ds(pl.multiple_of(chip * 24, 8), 24), :] = lines[outer][inner, :, lanes]


def factor_kernel(place_ref, l0, l1, l2, l3, wa, wb, nba, cross, s):
    lines = (l0, l1, l2, l3)
    sort_tiles(place_ref, lines, s, slice(0, 384))
    s[...] = 0.5 * (s[...] + s[...].T)
    panel_inverse(s, wa)
    sort_tiles(place_ref, lines, cross, slice(384, 768))
    nba[...] = nn(wa[...], cross[...])
    sort_tiles(place_ref, lines, s, slice(768, 1152))
    s[...] = 0.5 * (s[...] + s[...].T) - tn(nba[...], nba[...])
    panel_inverse(s, wb)


def factors(where, lines):
    square = jax.ShapeDtypeStruct((384, 384), jnp.float32)
    return pl.pallas_call(
        factor_kernel,
        out_shape=(square,) * 3,
        in_specs=[smem()] + [vmem()] * 4,
        out_specs=(vmem(),) * 3,
        scratch_shapes=[VMEM((384, 384), jnp.float32), VMEM((384, 384), jnp.float32)],
        compiler_params=params(),
        cost_estimate=cost(2 * 40 * 384 * 384 * 768, 20 * 384 * 384),
        name="pivot_factors",
    )(where, *lines)


def finish_kernel(place_ref, r0, r1, r2, r3, wa_ref, wb_ref, nba_ref, p0, p1, p2, p3, new):
    total = (r0[...] + r1[...]) + (r2[...] + r3[...])
    new_a = nt(wa_ref[...], total[:, :384])
    new[:384, :] = new_a
    new[384:, :] = nt(wb_ref[...], total[:, 384:] - tn(new_a, nba_ref[...]))
    for hop, out in zip(COMES_FROM, (p0, p1, p2, p3)):
        start = lax.rem(place_ref[3] + hop, 4) * 96
        for panel in range(2):
            rows = pl.ds(pl.multiple_of(384 * panel + start, 32), 96)
            out[96 * panel : 96 * panel + 96, :] = new[rows, :]


def finish(where, parts, wa, wb, nba):
    size = parts[0].shape[0]
    return pl.pallas_call(
        finish_kernel,
        out_shape=(jax.ShapeDtypeStruct((192, size), jnp.float32),) * 4,
        in_specs=[smem()] + [vmem()] * 7,
        out_specs=(vmem(),) * 4,
        scratch_shapes=[VMEM((768, size), jnp.float32)],
        compiler_params=params(),
        cost_estimate=cost(2 * 6 * size * 384 * 384 * 3, 4 * size * 768 * 6),
        name="new_vectors",
    )(where, *parts, wa, wb, nba)


def join_kernel(place_ref, p0, p1, p2, p3, out_a, out_b):
    size = p0.shape[1]
    for hop, piece in zip(COMES_FROM, (p0, p1, p2, p3)):
        lanes = pl.ds(pl.multiple_of(lax.rem(place_ref[3] + 4 - hop, 4) * size, size), size)
        out_a[:, lanes] = piece[:96, :]
        out_b[:, lanes] = piece[96:, :]


def join(where, pieces):
    out = jax.ShapeDtypeStruct((96, 4 * pieces[0].shape[1]), jnp.float32)
    return pl.pallas_call(
        join_kernel,
        out_shape=(out, out),
        in_specs=[smem()] + [vmem()] * 4,
        out_specs=(vmem(), vmem()),
        compiler_params=params(),
        name="join_vectors",
    )(where, *pieces)


def to_group(array, hop):
    return lax.ppermute(array, "grp", [(g, (g + hop) % 4) for g in range(4)])


def body(vectors, column_a, column_b, pivot_a, pivot_b):
    rows_here = vectors.shape[0]
    place_here = lax.axis_index("rows")
    group = lax.axis_index("grp")
    core = place_here % 2
    where = jnp.stack([place_here // 8, (place_here // 2) % 4, core, group]).astype(jnp.int32)

    pivots = jnp.concatenate([pivot_a, pivot_b])
    owner, local = pivots // rows_here, pivots % rows_here
    index = lax.iota(jnp.int32, 768)
    same = (owner[:, None] == owner[None, :]) & (index[:, None] > index[None, :])
    rank = jnp.sum(same.astype(jnp.int32), axis=1)
    rounds = jnp.max(rank) // CAP + 1

    def send(turn):
        slots = turn * CAP + lax.iota(jnp.int32, CAP)
        hit = (owner == place_here)[None, :] & (rank[None, :] == slots[:, None])
        rows = jnp.sum(jnp.where(hit, local[None, :], 0), axis=1)
        return lax.all_to_all(pick(rows, vectors, column_a, column_b), "rows", 0, 0)

    def take(turn, got):
        return place(jnp.stack([owner, jnp.clip(rank - turn * CAP, 0, CAP - 1)]), got)

    def more(state):
        turn, block, colt = state
        new_block, new_colt = take(turn, send(turn))
        now = rank // CAP == turn
        wide = jnp.where(lax.iota(jnp.int32, 128)[None, :] < 64, now[:384, None], now[384:, None])
        return turn + 1, jnp.where(wide, new_block, block), jnp.where(now[None, :], new_colt, colt)

    got = send(0)
    vhigh, vlow = split_rows(vectors)
    got, vhigh, vlow = lax.optimization_barrier((got, vhigh, vlow))
    block, colt = take(0, got)
    _, block, colt = lax.while_loop(lambda state: state[0] < rounds, more, (jnp.int32(1), block, colt))

    line = first_ring(block)
    near, next_to, far = share(where, line, colt)
    far = lax.ppermute(far, "rows", paired("y", 2))
    lines = second_ring(line)
    tile = (near + far[0]) + lax.ppermute(next_to + far[1], "rows", paired("y", 1))
    tile = tile + other_core(tile)
    for bit in (1, 2):
        tile = tile + lax.ppermute(tile, "grp", [(g, g ^ bit) for g in range(4)])
    swapped = [other_core(line) for line in lines]
    pair = jnp.stack([tile, lax.ppermute(tile, "rows", paired("x", 1))])
    row = jnp.concatenate([pair, lax.ppermute(pair, "rows", paired("x", 2))])
    parts = product(where, vhigh, vlow, column_a, column_b, lines + swapped)
    row, *parts = lax.optimization_barrier((row, *parts))
    tiles = second_ring(row)
    total = [parts[0]] + [to_group(part, hop) for hop, part in zip(COMES_FROM[1:], parts[1:])]

    wa, wb, nba = factors(where, tiles)
    pieces = finish(where, total, wa, wb, nba)
    pieces = [pieces[0]] + [to_group(piece, hop) for hop, piece in zip(COMES_FROM[1:], pieces[1:])]
    out_a, out_b = join(where, pieces)
    return out_a.T, out_b.T


def solution(mesh):
    in_specs = (P("rows", "grp"), P("rows", None), P("rows", None), P(), P())
    out_specs = (P("rows", "grp"), P("rows", "grp"))
    return jax.shard_map(body, mesh=mesh, in_specs=in_specs, out_specs=out_specs, check_vma=False)
```

```python
import functools

import jax
import jax.numpy as jnp
from jax import lax
from jax.experimental import pallas as pl
from jax.experimental.pallas import tpu as pltpu
from jax.sharding import PartitionSpec as P

HIGHEST = lax.Precision.HIGHEST
CAP = 48
COMES_FROM = (0, 1, 3, 2)
VMEM = pltpu.VMEM
LIMIT = 50 * 1024 * 1024


def vmem():
    return pl.BlockSpec(memory_space=VMEM)


def smem():
    return pl.BlockSpec(memory_space=pltpu.SMEM)


def params():
    return pltpu.CompilerParams(vmem_limit_bytes=LIMIT)


def cost(flops, byte_count):
    return pl.CostEstimate(flops=flops, bytes_accessed=byte_count, transcendentals=0)


def nt(left, right, precision=HIGHEST):
    return lax.dot_general(
        left, right, (((1,), (1,)), ((), ())), precision=precision, preferred_element_type=jnp.float32
    )


def nn(left, right):
    return lax.dot_general(
        left, right, (((1,), (0,)), ((), ())), precision=HIGHEST, preferred_element_type=jnp.float32
    )


def tn(left, right):
    return lax.dot_general(
        left, right, (((0,), (0,)), ((), ())), precision=HIGHEST, preferred_element_type=jnp.float32
    )


def pick_kernel(rows_ref, v_ref, ca_ref, cb_ref, out_ref, vbuf, abuf, bbuf, sems):
    count = vbuf.shape[0]

    @pl.loop(0, count)
    def _(slot):
        row = rows_ref[slot]
        pltpu.make_async_copy(v_ref.at[pl.ds(row, 1)], vbuf.at[pl.ds(slot, 1)], sems.at[0]).start()
        pltpu.make_async_copy(ca_ref.at[pl.ds(row, 1)], abuf.at[pl.ds(slot, 1)], sems.at[1]).start()
        pltpu.make_async_copy(cb_ref.at[pl.ds(row, 1)], bbuf.at[pl.ds(slot, 1)], sems.at[2]).start()

    pltpu.make_async_copy(vbuf, vbuf, sems.at[0]).wait()
    pltpu.make_async_copy(abuf, abuf, sems.at[1]).wait()
    pltpu.make_async_copy(bbuf, bbuf, sems.at[2]).wait()
    gap = jnp.zeros((CAP, 40), jnp.float32)
    for c in range(16):
        for q, column in enumerate((abuf, bbuf)):
            start = 128 * c + 64 * q
            out_ref[2 * c + q] = jnp.concatenate(
                [vbuf[:, start : start + 64], column[:, 24 * c : 24 * c + 24], gap], axis=1
            )


def pick(rows, vectors, column_a, column_b):
    width = vectors.shape[1]
    anywhere = pl.BlockSpec(memory_space=pl.ANY)
    return pl.pallas_call(
        pick_kernel,
        out_shape=jax.ShapeDtypeStruct((32, CAP, 128), jnp.float32),
        in_specs=[smem(), anywhere, anywhere, anywhere],
        out_specs=vmem(),
        scratch_shapes=[
            VMEM((CAP, width), jnp.float32),
            VMEM((CAP, 384), jnp.float32),
            VMEM((CAP, 384), jnp.float32),
            pltpu.SemaphoreType.DMA((3,)),
        ],
        compiler_params=params(),
        name="pick_rows",
    )(rows, vectors, column_a, column_b)


def place_kernel(pos_ref, got_ref, x_ref, colt_ref, buf):
    @pl.loop(0, 768, unroll=8)
    def _(i):
        buf[pl.ds(i, 1), :] = got_ref[pos_ref[0, i], pl.ds(pos_ref[1, i], 1), :]

    x_ref[...] = jnp.concatenate([buf[:384, :64], buf[384:, :64]], axis=1)
    colt_ref[...] = buf[:, 64:88].T


def place(pos, got):
    return pl.pallas_call(
        place_kernel,
        out_shape=(
            jax.ShapeDtypeStruct((384, 128), jnp.float32),
            jax.ShapeDtypeStruct((24, 768), jnp.float32),
        ),
        in_specs=[smem(), vmem()],
        out_specs=(vmem(), vmem()),
        scratch_shapes=[VMEM((768, 128), jnp.float32)],
        compiler_params=params(),
        name="place_rows",
    )(pos, got)


def turned(axis, step):
    def to(index):
        y, x, core = index // 8, (index // 2) % 4, index % 2
        along_x = axis == "x" if core == 0 else axis == "y"
        if along_x:
            x = (x + step) % 4
        else:
            y = (y + step) % 4
        return (y * 4 + x) * 2 + core

    return [(index, to(index)) for index in range(32)]


def paired(axis, bit):
    def to(index):
        y, x, core = index // 8, (index // 2) % 4, index % 2
        along_x = axis == "x" if core == 0 else axis == "y"
        return ((y * 4 + (x ^ bit)) if along_x else ((y ^ bit) * 4 + x)) * 2 + core

    return [(index, to(index)) for index in range(32)]


def other_core(array):
    return lax.ppermute(array, "rows", [(index, index ^ 1) for index in range(32)])


def first_ring(block):
    return jnp.stack([block] + [lax.ppermute(block, "rows", turned("x", step)) for step in COMES_FROM[1:]])


def second_ring(line):
    return [line] + [lax.ppermute(line, "rows", turned("y", step)) for step in COMES_FROM[1:]]


def flipped(value, bit):
    low = value + (bit % 2) * (1 - 2 * lax.rem(value, 2))
    return lax.rem(low + 2 * (bit // 2), 4)


def spot_flipped(place_ref, outer, inner):
    y, x, core = place_ref[0], place_ref[1], place_ref[2]
    at_x = jnp.where(core == 0, flipped(x, inner), lax.rem(x + 4 - outer, 4))
    at_y = jnp.where(core == 0, lax.rem(y + 4 - outer, 4), flipped(y, inner))
    return at_y * 4 + at_x


def spot(place_ref, outer, inner):
    y, x, core = place_ref[0], place_ref[1], place_ref[2]
    dx = jnp.where(core == 0, inner, outer)
    dy = jnp.where(core == 0, outer, inner)
    return lax.rem(y + 4 - dy, 4) * 4 + lax.rem(x + 4 - dx, 4)


def share_kernel(place_ref, line_ref, colt_ref, o0, o1, o2, o3, first, second):
    for piece in range(4):
        value = line_ref[piece]
        first[:, 64 * piece : 64 * piece + 64] = value[:, :64]
        second[:, 64 * piece : 64 * piece + 64] = value[:, 64:]
    rows_a, rows_b = [], []
    core = place_ref[2]
    for hop in COMES_FROM:
        rows = pl.ds(pl.multiple_of(spot(place_ref, 4 - hop, 0) * 24, 8), 24)
        rows_a.append(first[rows, :])
        rows_b.append(second[rows, :])
    rows_a, rows_b = jnp.concatenate(rows_a, axis=0), jnp.concatenate(rows_b, axis=0)
    aa, ab, bb = nt(rows_a, first[...]), nt(rows_a, second[...]), nt(rows_b, second[...])
    for number, out in enumerate((o0, o1, o2, o3)):
        some = slice(24 * number, 24 * number + 24)
        out[:, :384] = -aa[some]
        out[:, 384:768] = -ab[some]
        out[:, 768:] = -bb[some]

    @pl.when(core == 0)
    def _():
        o0[:, :768] += 0.25 * colt_ref[...]

    @pl.when(core == 1)
    def _():
        o0[:, 768:] += 0.25 * colt_ref[:, 384:]


def share(where, line, colt):
    return pl.pallas_call(
        share_kernel,
        out_shape=(jax.ShapeDtypeStruct((24, 1152), jnp.float32),) * 4,
        in_specs=[smem(), vmem(), vmem()],
        out_specs=(vmem(),) * 4,
        scratch_shapes=[VMEM((384, 256), jnp.float32), VMEM((384, 256), jnp.float32)],
        compiler_params=params(),
        cost_estimate=cost(2 * 96 * 1152 * 256 * 24, 4 * 384 * 512),
        name="pivot_share",
    )(where, line, colt)


def split(value):
    high = value.astype(jnp.bfloat16)
    return high, (value - high.astype(jnp.float32)).astype(jnp.bfloat16)


def order_rows(place_ref, own, sibling, high_ref, low_ref):
    for outer in range(4):
        for inner in range(4):
            lanes = pl.ds(pl.multiple_of(spot(place_ref, COMES_FROM[outer], COMES_FROM[inner]) * 128, 128), 128)
            mine, theirs = own[outer][inner], sibling[inner][outer]
            low_core = jnp.where(place_ref[2] == 0, mine, theirs)
            high_core = jnp.where(place_ref[2] == 0, theirs, mine)
            for panel in range(2):
                half = slice(64 * panel, 64 * panel + 64)
                tile = jnp.concatenate([low_core[:, half], high_core[:, half]], axis=1)
                rows = slice(384 * panel, 384 * panel + 384)
                high_ref[rows, lanes], low_ref[rows, lanes] = split(tile)


def split_kernel(v_ref, high_ref, low_ref):
    high_ref[...], low_ref[...] = split(v_ref[...])


def split_rows(vectors):
    rows, width = vectors.shape
    block = pl.BlockSpec((rows // 8, width), lambda n: (n, 0))
    half = jax.ShapeDtypeStruct((rows, width), jnp.bfloat16)
    return pl.pallas_call(
        split_kernel,
        out_shape=(half, half),
        grid=(8,),
        in_specs=[block],
        out_specs=(block, block),
        compiler_params=params(),
        cost_estimate=cost(4 * rows * width, 8 * rows * width),
        name="split_vectors",
    )(vectors)


def product_kernel(place_ref, vhigh, vlow, ca_ref, cb_ref, *refs):
    own, sibling, outs, high_ref, low_ref = refs[:4], refs[4:8], refs[8:12], refs[12], refs[13]
    step = pl.program_id(0)

    @pl.when(step == 0)
    def _():
        order_rows(place_ref, own, sibling, high_ref, low_ref)

    total = nt(vhigh[...], high_ref[...], None)
    total += nt(vhigh[...], low_ref[...], None)
    total += nt(vlow[...], high_ref[...], None)
    for number, out in enumerate(outs):

        @pl.when(step == number)
        def _():
            out[:, :384] = 0.25 * ca_ref[...] - total[:, :384]
            out[:, 384:] = 0.25 * cb_ref[...] - total[:, 384:]


def product(where, vhigh, vlow, column_a, column_b, lines):
    rows, width = vhigh.shape
    size = rows // 4

    def chunk(n, place):
        hop = jnp.where(n < 2, n, 5 - n)
        return lax.rem(place[3] + hop, 4), 0

    whole = pl.BlockSpec(lines[0].shape, lambda n, place: (0, 0, 0))
    return pl.pallas_call(
        product_kernel,
        out_shape=(jax.ShapeDtypeStruct((size, 768), jnp.float32),) * 4,
        grid_spec=pltpu.PrefetchScalarGridSpec(
            num_scalar_prefetch=1,
            grid=(4,),
            in_specs=[
                pl.BlockSpec((size, width), chunk),
                pl.BlockSpec((size, width), chunk),
                pl.BlockSpec((size, 384), chunk),
                pl.BlockSpec((size, 384), chunk),
            ]
            + [whole] * 8,
            out_specs=(pl.BlockSpec((size, 768), lambda n, place: (0, 0)),) * 4,
            scratch_shapes=[VMEM((768, width), jnp.bfloat16), VMEM((768, width), jnp.bfloat16)],
        ),
        compiler_params=params(),
        cost_estimate=cost(2 * 3 * rows * width * 768, 4 * rows * width + 4 * 768 * width),
        name="product_rows",
    )(where, vhigh, vlow, column_a, column_b, *lines)


def spread(row, index):
    return jnp.broadcast_to(row[index : index + 1, :], (8, 128))


def invert_factor(a):
    row_of = lax.broadcasted_iota(jnp.int32, (8, 128), 0)
    lane_of = lax.broadcasted_iota(jnp.int32, (8, 128), 1)
    e = [jnp.where(lane_of == row_of + 8 * j, 1.0, 0.0) for j in range(16)]
    done = []
    for j in range(16):
        rest = range(j, 16)
        cols = {
            (s, i): jnp.broadcast_to(a[s][:, 8 * j + i : 8 * j + i + 1], (8, 128)) for s in rest for i in range(8)
        }
        diagonal = jnp.ones((8, 128), jnp.float32)
        for i in range(8):
            pivot = spread(cols[(j, i)], i)
            diagonal = jnp.where(row_of == i, pivot, diagonal)
            inverse = 1.0 / pivot
            factor = {s: cols[(s, i)] * inverse for s in rest}
            factor[j] = jnp.where(row_of > i, factor[j], 0.0)
            for later in range(i + 1, 8):
                head = spread(cols[(j, later)], i)
                for s in rest:
                    cols[(s, later)] = cols[(s, later)] - factor[s] * head
            head_a, head_e = spread(a[j], i), spread(e[j], i)
            for s in rest:
                a[s] = a[s] - factor[s] * head_a
                e[s] = e[s] - factor[s] * head_e
        done.append(e[j] * lax.rsqrt(diagonal))
    return done


def panel_inverse(s, w):
    w[...] = jnp.zeros_like(w)
    for b in range(3):
        here = slice(128 * b, 128 * b + 128)
        strips = invert_factor([s[128 * b + 8 * j : 128 * b + 8 * j + 8, here] for j in range(16)])
        for j in range(16):
            w[128 * b + 8 * j : 128 * b + 8 * j + 8, here] = strips[j]
        inverse = w[here, here]
        if b:
            w[here, : 128 * b] = nn(inverse, w[here, : 128 * b])
        if b < 2:
            below = slice(128 * b + 128, 384)
            left = nt(s[below, here], inverse)
            s[below, below] = s[below, below] - nt(left, left)
            w[below, : 128 * b + 128] = w[below, : 128 * b + 128] - nn(left, w[here, : 128 * b + 128])


def sort_tiles(place_ref, lines, st, lanes):
    for outer in range(4):
        for inner in range(4):
            chip = spot_flipped(place_ref, COMES_FROM[outer], inner)
            st[pl.ds(pl.multiple_of(chip * 24, 8), 24), :] = lines[outer][inner, :, lanes]


def factor_kernel(place_ref, l0, l1, l2, l3, wa, wb, nba, cross, s):
    lines = (l0, l1, l2, l3)
    sort_tiles(place_ref, lines, s, slice(0, 384))
    s[...] = 0.5 * (s[...] + s[...].T)
    panel_inverse(s, wa)
    sort_tiles(place_ref, lines, cross, slice(384, 768))
    nba[...] = nn(wa[...], cross[...])
    sort_tiles(place_ref, lines, s, slice(768, 1152))
    s[...] = 0.5 * (s[...] + s[...].T) - tn(nba[...], nba[...])
    panel_inverse(s, wb)


def factors(where, lines):
    square = jax.ShapeDtypeStruct((384, 384), jnp.float32)
    return pl.pallas_call(
        factor_kernel,
        out_shape=(square,) * 3,
        in_specs=[smem()] + [vmem()] * 4,
        out_specs=(vmem(),) * 3,
        scratch_shapes=[VMEM((384, 384), jnp.float32), VMEM((384, 384), jnp.float32)],
        compiler_params=params(),
        cost_estimate=cost(2 * 40 * 384 * 384 * 768, 20 * 384 * 384),
        name="pivot_factors",
    )(where, *lines)


def finish_kernel(place_ref, r0, r1, r2, r3, wa_ref, wb_ref, nba_ref, p0, p1, p2, p3, new):
    total = (r0[...] + r1[...]) + (r2[...] + r3[...])
    new_a = nt(wa_ref[...], total[:, :384])
    new[:384, :] = new_a
    new[384:, :] = nt(wb_ref[...], total[:, 384:] - tn(new_a, nba_ref[...]))
    for hop, out in zip(COMES_FROM, (p0, p1, p2, p3)):
        start = lax.rem(place_ref[3] + hop, 4) * 96
        for panel in range(2):
            rows = pl.ds(pl.multiple_of(384 * panel + start, 32), 96)
            out[96 * panel : 96 * panel + 96, :] = new[rows, :]


def finish(where, parts, wa, wb, nba):
    size = parts[0].shape[0]
    return pl.pallas_call(
        finish_kernel,
        out_shape=(jax.ShapeDtypeStruct((192, size), jnp.float32),) * 4,
        in_specs=[smem()] + [vmem()] * 7,
        out_specs=(vmem(),) * 4,
        scratch_shapes=[VMEM((768, size), jnp.float32)],
        compiler_params=params(),
        cost_estimate=cost(2 * 6 * size * 384 * 384 * 3, 4 * size * 768 * 6),
        name="new_vectors",
    )(where, *parts, wa, wb, nba)


def join_kernel(place_ref, p0, p1, p2, p3, out_a, out_b):
    size = p0.shape[1]
    for hop, piece in zip(COMES_FROM, (p0, p1, p2, p3)):
        lanes = pl.ds(pl.multiple_of(lax.rem(place_ref[3] + 4 - hop, 4) * size, size), size)
        out_a[:, lanes] = piece[:96, :]
        out_b[:, lanes] = piece[96:, :]


def join(where, pieces):
    out = jax.ShapeDtypeStruct((96, 4 * pieces[0].shape[1]), jnp.float32)
    return pl.pallas_call(
        join_kernel,
        out_shape=(out, out),
        in_specs=[smem()] + [vmem()] * 4,
        out_specs=(vmem(), vmem()),
        compiler_params=params(),
        name="join_vectors",
    )(where, *pieces)


def to_group(array, hop):
    return lax.ppermute(array, "grp", [(g, (g + hop) % 4) for g in range(4)])


def body(vectors, column_a, column_b, pivot_a, pivot_b):
    rows_here = vectors.shape[0]
    place_here = lax.axis_index("rows")
    group = lax.axis_index("grp")
    core = place_here % 2
    where = jnp.stack([place_here // 8, (place_here // 2) % 4, core, group]).astype(jnp.int32)

    pivots = jnp.concatenate([pivot_a, pivot_b])
    owner, local = pivots // rows_here, pivots % rows_here
    index = lax.iota(jnp.int32, 768)
    same = (owner[:, None] == owner[None, :]) & (index[:, None] > index[None, :])
    rank = jnp.sum(same.astype(jnp.int32), axis=1)
    rounds = jnp.max(rank) // CAP + 1

    def send(turn):
        slots = turn * CAP + lax.iota(jnp.int32, CAP)
        hit = (owner == place_here)[None, :] & (rank[None, :] == slots[:, None])
        rows = jnp.sum(jnp.where(hit, local[None, :], 0), axis=1)
        return lax.all_to_all(pick(rows, vectors, column_a, column_b), "rows", 0, 0)

    def take(turn, got):
        return place(jnp.stack([owner, jnp.clip(rank - turn * CAP, 0, CAP - 1)]), got)

    def more(state):
        turn, block, colt = state
        new_block, new_colt = take(turn, send(turn))
        now = rank // CAP == turn
        wide = jnp.where(lax.iota(jnp.int32, 128)[None, :] < 64, now[:384, None], now[384:, None])
        return turn + 1, jnp.where(wide, new_block, block), jnp.where(now[None, :], new_colt, colt)

    got = send(0)
    vhigh, vlow = split_rows(vectors)
    got, vhigh, vlow = lax.optimization_barrier((got, vhigh, vlow))
    block, colt = take(0, got)
    _, block, colt = lax.while_loop(lambda state: state[0] < rounds, more, (jnp.int32(1), block, colt))

    line = first_ring(block)
    shares = share(where, line, colt)
    line, *shares = lax.optimization_barrier((line, *shares))
    tile = shares[0]
    for hop, piece in zip(COMES_FROM[1:], shares[1:]):
        tile = tile + lax.ppermute(piece, "rows", turned("y", hop))
    lines = second_ring(line)
    tile = tile + other_core(tile)
    for bit in (1, 2):
        tile = tile + lax.ppermute(tile, "grp", [(g, g ^ bit) for g in range(4)])
    swapped = [other_core(line) for line in lines]
    pair = jnp.stack([tile, lax.ppermute(tile, "rows", paired("x", 1))])
    row = jnp.concatenate([pair, lax.ppermute(pair, "rows", paired("x", 2))])
    parts = product(where, vhigh, vlow, column_a, column_b, lines + swapped)
    row, *parts = lax.optimization_barrier((row, *parts))
    tiles = second_ring(row)
    total = [parts[0]] + [to_group(part, hop) for hop, part in zip(COMES_FROM[1:], parts[1:])]

    wa, wb, nba = factors(where, tiles)
    pieces = finish(where, total, wa, wb, nba)
    pieces = [pieces[0]] + [to_group(piece, hop) for hop, piece in zip(COMES_FROM[1:], pieces[1:])]
    out_a, out_b = join(where, pieces)
    return out_a.T, out_b.T


def solution(mesh):
    in_specs = (P("rows", "grp"), P("rows", None), P("rows", None), P(), P())
    out_specs = (P("rows", "grp"), P("rows", "grp"))
    return jax.shard_map(body, mesh=mesh, in_specs=in_specs, out_specs=out_specs, check_vma=False)
```
